256 devices in a mesh: seq: 32 (over x, z), head: 8 (over y, core).
Axes of the slice: x: 4, y: 4, z: 8, core: 2. Of those that a mesh axis runs over, the one named last changes fastest.
Arguments:
- tokens: bfloat16 [8192, 4096], P('seq', 'head'), may hold values from -6 to 6
- neighbour_shard: int32 [128, 2], P('seq'), may hold values from 0 to 31, as said below
- neighbour_row: int32 [128, 2], P('seq'), may hold values from 0 to 15
- store_rows: bfloat16 [512, 128, 896], P('seq'), may hold values from -6 to 6
- context_weight: bfloat16 [4096, 896], P('head'), may hold values from -0.1875 to 0.1875
- query_weight: bfloat16 [4096, 2048], P(None, 'head'), may hold values from -0.09375 to 0.09375
- key_weight: bfloat16 [896, 2048], P(None, 'head'), may hold values from -0.25 to 0.25
- value_weight: bfloat16 [896, 2048], P(None, 'head'), may hold values from -0.1875 to 0.1875
- output_weight: bfloat16 [2048, 4096], P(None, 'head'), may hold values from -0.25 to 0.25
Outputs:
- attended: bfloat16 [8192, 4096], P('seq', 'head')
The draws below stay inside these ranges and needn't reach their ends.
Inputs may be any that keep to these rules, and one draw needn't show every extreme that they name: `neighbour_shard`: among the 8 neighbours of the spans of one seq index, at most 2 lie in any one store shard; in every draw one shard holds exactly 2 neighbours of every seq index's spans.
All inputs are finite; a program needn't handle non-finite values.
Results may differ from the reference program's by a relative error of at most 0.015.
The reference program's roundings to bfloat16 on the way count: a program that leaves them out, or rounds other values in their place, can miss the bound.
Values may be sent and summed in bfloat16 or wider, within the bound.
No kernel may reach another device: no remote copies, remote signals or barrier semaphores. Data moves between devices by JAX's collectives and lax.ppermute only.
A program may use at most 192 MiB of HBM per device.

```python
import math
import jax
import jax.numpy as jnp
from jax import lax

D = 4096
H = 16
HD = 128
E = 896
CL = 64
NL = 128
KN = 2
EHD = 128
STORE_DEV = 16
CH_DEV = 4
TOKENS = 8192
SPANS = 128
STORE = 512
CAP = 2
N_SEQ = 32


def draw_neighbour_shard(key, part):
    key = jax.random.fold_in(key, 11)
    requests = CH_DEV * KN
    hot_key, rest_key = jax.random.split(key)
    hot_owner = jax.random.randint(hot_key, (), 0, N_SEQ)
    source_keys = jax.random.split(rest_key, N_SEQ)

    def per_source(source_key):
        order_key, other_key, offset_key = jax.random.split(source_key, 3)
        order_perm = jax.random.permutation(order_key, requests)
        others_perm = jax.random.permutation(other_key, N_SEQ - 1)
        offset_bit = jax.random.randint(offset_key, (), 0, 2)
        position = jnp.arange(requests - CAP)
        group_index = jnp.minimum((position + offset_bit) // CAP, N_SEQ - 2)
        others = (hot_owner + 1 + others_perm[group_index]) % N_SEQ
        owners = jnp.concatenate([jnp.full((CAP,), hot_owner, jnp.int32), others.astype(jnp.int32)])
        return owners[order_perm]
    everything = jax.vmap(per_source)(source_keys)
    return everything.reshape(SPANS, KN).astype(jnp.int32)


def touch_ends(drawn, stream_key, low, high):
    longest = drawn.shape.index(max(drawn.shape))
    spots = []
    for shift in (0, 1):
        where = [jax.random.randint(jax.random.fold_in(stream_key, axis), (), 0, length) for axis, length in enumerate(drawn.shape)]
        where[longest] = (where[longest] + shift) % drawn.shape[longest]
        spots.append(tuple(where))
    return drawn.at[spots[0]].set(low).at[spots[1]].set(high)


def steps_of(stream_key, shape, shards, smallest, top_value):
    factor_of, own = 1.0, jax.random.fold_in(stream_key, 6)
    for dim, blocks in shards:
        steps = jnp.exp(jax.random.uniform(jax.random.fold_in(own, dim), (blocks,), jnp.float32, smallest / len(shards), top_value / len(shards)))
        factor_of = factor_of * jnp.repeat(steps, shape[dim] // blocks).reshape([-1 if axis == dim else 1 for axis in range(len(shape))])
    return factor_of


def centred(stream_key, dims, scale, bound, cuts=(), dtype=jnp.bfloat16):
    entries = scale * jax.random.normal(stream_key, dims, jnp.float32)
    if cuts:
        entries = entries * steps_of(stream_key, dims, cuts, -0.22, 0.18)
    return jnp.clip(entries, -bound, bound).astype(dtype)


def setup_inputs(seed: int = 0) -> dict:
    seeds = jax.random.split(jax.random.key(seed), 10)
    return {
        "tokens": centred(seeds[0], (TOKENS, D), 1.0, 6.0, ((0, 32), (1, 8))),
        "neighbour_shard": draw_neighbour_shard(jax.random.fold_in(seeds[9], 71), 0),
        "neighbour_row": touch_ends(jax.random.randint(seeds[2], (SPANS, KN), 0, STORE_DEV), jax.random.fold_in(seeds[2], 1), 0, STORE_DEV - 1).astype(jnp.int32),
        "store_rows": centred(seeds[3], (STORE, NL, E), 1.0, 6.0, ((0, 32),)),
        "context_weight": centred(seeds[4], (D, E), (D // 4) ** -0.5, 0.1875, ((0, 8),)),
        "query_weight": centred(seeds[5], (D, H * HD), D ** -0.5, 0.09375, ((1, 8),)),
        "key_weight": centred(seeds[6], (E, H * HD), (E // 2) ** -0.5, 0.25, ((1, 8),)),
        "value_weight": centred(seeds[7], (E, H * HD), E ** -0.5, 0.1875, ((1, 8),)),
        "output_weight": centred(seeds[8], (H * HD, D), (H * HD // 4) ** -0.5, 0.25, ((1, 8),)),
    }


def encode(neighbour, context):
    batch_count = neighbour.shape[0]
    head_count = E // EHD
    query_side = neighbour.astype(jnp.float32).reshape(batch_count, NL, head_count, EHD)
    key_side = context.astype(jnp.float32).reshape(batch_count, CL, head_count, EHD)
    scores = jnp.einsum('nkgd,nqgd->ngkq', key_side, query_side) * (1.0 / math.sqrt(EHD))
    weights = jnp.exp(scores - lax.optimization_barrier(jnp.max(scores, axis=2, keepdims=True)))
    weights = (weights / lax.optimization_barrier(jnp.sum(weights, axis=2, keepdims=True))).astype(jnp.bfloat16)
    mixed_in = jnp.einsum('ngkq,nkgd->nqgd', weights.astype(jnp.float32), key_side)
    return (neighbour.astype(jnp.float32) + mixed_in.reshape(batch_count, NL, E)).astype(jnp.bfloat16)

def reference(tokens, neighbour_shard, neighbour_row, store_rows, context_weight, query_weight, key_weight, value_weight, output_weight):
    context = jnp.dot(tokens, context_weight, preferred_element_type=jnp.float32).astype(jnp.bfloat16).reshape(SPANS, CL, E)
    queries = jnp.dot(tokens, query_weight, preferred_element_type=jnp.float32).astype(jnp.bfloat16).reshape(SPANS, CL, H, HD)
    lookup = (neighbour_shard * STORE_DEV + neighbour_row).astype(jnp.int32)

    def per_span(span_items):
        context_one, queries_one, lookup_one = span_items
        neighbour = jnp.take(store_rows, lookup_one, axis=0)
        encoded = encode(neighbour, jnp.broadcast_to(context_one, (KN, CL, E)))
        flat_rows = encoded.reshape(KN * NL, E)
        keys_all = jnp.dot(flat_rows, key_weight, preferred_element_type=jnp.float32).astype(jnp.bfloat16).reshape(KN * NL, H, HD)
        values_all = jnp.dot(flat_rows, value_weight, preferred_element_type=jnp.float32).astype(jnp.bfloat16).reshape(KN * NL, H, HD)
        scores = jnp.einsum('qhd,khd->hqk', queries_one.astype(jnp.float32), keys_all.astype(jnp.float32)) * (1.0 / math.sqrt(HD))
        weights = jnp.exp(scores - lax.optimization_barrier(jnp.max(scores, axis=-1, keepdims=True)))
        weights = (weights / lax.optimization_barrier(jnp.sum(weights, axis=-1, keepdims=True))).astype(jnp.bfloat16)
        result = jnp.einsum('hqk,khd->qhd', weights.astype(jnp.float32), values_all.astype(jnp.float32))
        return result.reshape(CL, H * HD).astype(jnp.bfloat16)
    attention = lax.map(per_span, (context, queries, lookup)).reshape(TOKENS, H * HD)
    return jnp.dot(attention, output_weight, preferred_element_type=jnp.float32).astype(jnp.bfloat16)
```

```python
import functools
import math

import jax
import jax.numpy as jnp
from jax import lax
from jax.experimental import pallas as pl
from jax.experimental.pallas import tpu as pltpu
from jax.sharding import PartitionSpec as P

HD = 128
E = 896
CL = 64
NL = 128
KN = 2
EHD = 128
NX, NZ, NY, NC = 4, 8, 4, 2
NS = NX * NZ
NH = NY * NC
CAP = 2
ROWS = NL // NH
BF = jnp.bfloat16
F32 = jnp.float32


def y_shift(a, r):
    pairs = [(y * NC + c, ((y + r) % NY) * NC + c) for y in range(NY) for c in range(NC)]
    return lax.ppermute(a, "head", pairs)


def core_swap(a):
    return lax.ppermute(a, "head", [(h, h ^ 1) for h in range(NH)])


def head_blocks(a):
    own = [a] + [y_shift(a, r) for r in (1, 3, 2)]
    own = [own[0], own[1], own[3], own[2]]
    return [(b, core_swap(b)) for b in own]


def block_order(y, c):
    return jnp.stack(
        [((y - r) % NY) * NC + (c if s == 0 else 1 - c) for r in range(NY) for s in range(NC)]
    ).astype(jnp.int32)


def blocked_dot_kernel(depth, order, *refs):
    blocks, w, out = refs[:NH], refs[NH], refs[NH + 1]
    total = None
    for k in range(NH):
        start = pl.multiple_of(order[k] * depth, depth)
        part = jnp.dot(blocks[k][...], w[pl.ds(start, depth), :], preferred_element_type=F32)
        total = part if total is None else total + part
    out[...] = total.astype(out.dtype)


def blocked_dot(blocks, order, w, name):
    rows, depth = blocks[0].shape
    width = w.shape[1]
    vmem = pl.BlockSpec(memory_space=pltpu.VMEM)
    return pl.pallas_call(
        functools.partial(blocked_dot_kernel, depth),
        out_shape=jax.ShapeDtypeStruct((rows, width), BF),
        in_specs=[pl.BlockSpec(memory_space=pltpu.SMEM)] + [vmem] * (NH + 1),
        out_specs=vmem,
        compiler_params=pltpu.CompilerParams(vmem_limit_bytes=24 * 2**20),
        cost_estimate=pl.CostEstimate(
            flops=2 * rows * depth * NH * width,
            bytes_accessed=2 * (rows * depth * NH + depth * NH * width + rows * width),
            transcendentals=0,
        ),
        name=name,
    )(order, *blocks, w)


def encode_kernel(order, nb, *refs):
    ctx, out = refs[: NY * NC], refs[NY * NC]
    heads = E // EHD
    for r in range(NY):
        span = order[NC * r] // NC
        context = jnp.concatenate([ctx[NC * r][...], ctx[NC * r + 1][...]], axis=0)
        rows = nb[pl.ds(span * KN, KN)].reshape(KN * ROWS, E)
        scores = jnp.concatenate(
            [
                lax.dot_general(
                    rows[:, g * EHD : (g + 1) * EHD],
                    context[:, g * EHD : (g + 1) * EHD],
                    (((1,), (1,)), ((), ())),
                    preferred_element_type=F32,
                )
                for g in range(heads)
            ],
            axis=0,
        ) * (1.0 / math.sqrt(EHD))
        weights = jnp.exp(scores - jnp.max(scores, axis=1, keepdims=True))
        weights = (weights / jnp.sum(weights, axis=1, keepdims=True)).astype(BF)
        mixed = jnp.concatenate(
            [
                jnp.dot(
                    weights[g * KN * ROWS : (g + 1) * KN * ROWS],
                    context[:, g * EHD : (g + 1) * EHD],
                    preferred_element_type=F32,
                )
                for g in range(heads)
            ],
            axis=1,
        )
        encoded = (rows.astype(F32) + mixed).astype(BF)
        out[pl.ds(span * KN, KN)] = encoded.reshape(KN, ROWS, E)


def encode(order, nb, ctx_blocks):
    vmem = pl.BlockSpec(memory_space=pltpu.VMEM)
    return pl.pallas_call(
        encode_kernel,
        out_shape=jax.ShapeDtypeStruct(nb.shape, BF),
        in_specs=[pl.BlockSpec(memory_space=pltpu.SMEM)] + [vmem] * (1 + NH),
        out_specs=vmem,
        compiler_params=pltpu.CompilerParams(vmem_limit_bytes=24 * 2**20),
        cost_estimate=pl.CostEstimate(
            flops=4 * nb.shape[0] * ROWS * CL * E,
            bytes_accessed=2 * 2 * nb.size + 2 * 256 * E,
            transcendentals=nb.shape[0] * ROWS * CL * 7,
        ),
        name="encode",
    )(order, nb, *ctx_blocks)


def attend_kernel(*refs):
    blocks = refs[:NH]
    q, wk, wv, out, rows, sems = refs[NH:]
    spans = rows.shape[0]
    copies = [
        pltpu.make_async_copy(blocks[b], rows.at[:, b], sems.at[b]) for b in range(NH)
    ]
    for copy in copies:
        copy.start()
    for copy in copies:
        copy.wait()
    flat = rows[...].reshape(spans * KN * NL, E)
    keys = jnp.dot(flat, wk[...], preferred_element_type=F32).astype(BF)
    values = jnp.dot(flat, wv[...], preferred_element_type=F32).astype(BF)
    heads = q.shape[1] // HD
    span_rows = KN * NL
    units = [(s, h) for s in range(spans) for h in range(heads)]
    scores = jnp.concatenate(
        [
            lax.dot_general(
                q[s * CL : (s + 1) * CL, h * HD : (h + 1) * HD],
                keys[s * span_rows : (s + 1) * span_rows, h * HD : (h + 1) * HD],
                (((1,), (1,)), ((), ())),
                preferred_element_type=F32,
            )
            for s, h in units
        ],
        axis=0,
    ) * (1.0 / math.sqrt(HD))
    weights = jnp.exp(scores - jnp.max(scores, axis=1, keepdims=True))
    weights = (weights / jnp.sum(weights, axis=1, keepdims=True)).astype(BF)
    for i, (s, h) in enumerate(units):
        out[s * CL : (s + 1) * CL, h * HD : (h + 1) * HD] = jnp.dot(
            weights[i * CL : (i + 1) * CL],
            values[s * span_rows : (s + 1) * span_rows, h * HD : (h + 1) * HD],
            preferred_element_type=F32,
        ).astype(BF)


def attend(blocks, queries, key_weight, value_weight):
    tokens, width = queries.shape
    spans = tokens // CL
    vmem = pl.BlockSpec(memory_space=pltpu.VMEM)
    blocks = [b.reshape(spans, KN * ROWS, E) for b in blocks]
    return pl.pallas_call(
        attend_kernel,
        out_shape=jax.ShapeDtypeStruct((tokens, width), BF),
        in_specs=[pl.BlockSpec(memory_space=pl.ANY)] * NH + [vmem] * 3,
        out_specs=vmem,
        scratch_shapes=[
            pltpu.VMEM((spans, NH, KN * ROWS, E), BF),
            pltpu.SemaphoreType.DMA((NH,)),
        ],
        compiler_params=pltpu.CompilerParams(vmem_limit_bytes=32 * 2**20),
        cost_estimate=pl.CostEstimate(
            flops=4 * spans * KN * NL * E * width + 4 * tokens * KN * NL * width,
            bytes_accessed=2 * (spans * KN * NL * E + 2 * E * width + 2 * tokens * width),
            transcendentals=tokens * KN * NL * 2,
        ),
        name="attend",
    )(*blocks, queries, key_weight, value_weight)


def sum_context(partial, y, c):
    parts = partial.reshape(NY, NC, -1, E)
    mine = lax.dynamic_index_in_dim(parts, c, axis=1, keepdims=False)
    theirs = lax.dynamic_index_in_dim(parts, 1 - c, axis=1, keepdims=False)
    chip = mine + core_swap(theirs)
    total = lax.dynamic_index_in_dim(chip, y, axis=0, keepdims=False)
    for r in (1, 3, 2):
        sent = lax.dynamic_index_in_dim(chip, (y + r) % NY, axis=0, keepdims=False)
        total = total + y_shift(sent, r)
    return total.astype(BF)


def fetch(store, neighbour_shard, neighbour_row, head):
    requests = neighbour_shard.size
    owners = neighbour_shard.reshape(requests)
    row_ids = neighbour_row.reshape(requests)
    hot = (owners[:, None] == jnp.arange(NS, dtype=jnp.int32)[None, :]).astype(jnp.int32)
    earlier = jnp.cumsum(hot, axis=0) - hot
    target = owners * CAP + jnp.sum(earlier * hot, axis=1)
    placing = target[None, :] == jnp.arange(NS * CAP, dtype=jnp.int32)[:, None]
    row_buffer = jnp.sum(placing.astype(jnp.int32) * row_ids[None, :], axis=1).reshape(NS, CAP)
    rows_in = lax.all_to_all(row_buffer, "seq", split_axis=0, concat_axis=0, tiled=True)
    slices = lax.dynamic_slice_in_dim(store, head * ROWS, ROWS, axis=1)
    sent = jnp.take(slices, rows_in.reshape(NS * CAP), axis=0)
    got = lax.all_to_all(sent, "seq", split_axis=0, concat_axis=0, tiled=True)
    return jnp.take(got, target, axis=0)


def local(
    tokens,
    neighbour_shard,
    neighbour_row,
    store_rows,
    context_weight,
    query_weight,
    key_weight,
    value_weight,
    output_weight,
):
    head = lax.axis_index("head")
    y, c = head // NC, head % NC
    order = block_order(y, c)
    neighbour = fetch(store_rows, neighbour_shard, neighbour_row, head)
    partial = jnp.dot(tokens, context_weight, preferred_element_type=F32)
    context = sum_context(partial, y, c)
    ctx_blocks = [b for pair in head_blocks(context) for b in pair]
    tok_blocks = [b for pair in head_blocks(tokens) for b in pair]
    queries = blocked_dot(tok_blocks, order, query_weight, "queries")
    encoded = encode(order, neighbour, ctx_blocks)
    enc_blocks = [b for pair in head_blocks(encoded) for b in pair]
    attention = attend(enc_blocks, queries, key_weight, value_weight)
    att_blocks = [b for pair in head_blocks(attention) for b in pair]
    return blocked_dot(att_blocks, order, output_weight, "project")


def solution(mesh):
    placed = (
        P("seq", "head"),
        P("seq", None),
        P("seq", None),
        P("seq", None, None),
        P("head", None),
        P(None, "head"),
        P(None, "head"),
        P(None, "head"),
        P(None, "head"),
    )
    return jax.shard_map(
        local, mesh=mesh, in_specs=placed, out_specs=P("seq", "head"), check_vma=False
    )
```

```python
import functools
import math

import jax
import jax.numpy as jnp
from jax import lax
from jax.experimental import pallas as pl
from jax.experimental.pallas import tpu as pltpu
from jax.sharding import PartitionSpec as P

HD = 128
E = 896
CL = 64
NL = 128
KN = 2
EHD = 128
NX, NZ, NY, NC = 4, 8, 4, 2
NS = NX * NZ
NH = NY * NC
STORE_DEV = 16
SLOTS = 8
CHUNKS = ((0, 7),)
ROWS = NL // NH
BF = jnp.bfloat16
F32 = jnp.float32


def y_shift(a, r):
    pairs = [(y * NC + c, ((y + r) % NY) * NC + c) for y in range(NY) for c in range(NC)]
    return lax.ppermute(a, "head", pairs)


def core_swap(a):
    return lax.ppermute(a, "head", [(h, h ^ 1) for h in range(NH)])


def head_blocks(a):
    own = [a] + [y_shift(a, r) for r in (1, 3, 2)]
    own = [own[0], own[1], own[3], own[2]]
    return [(b, core_swap(b)) for b in own]


def block_order(y, c):
    return jnp.stack(
        [((y - r) % NY) * NC + (c if s == 0 else 1 - c) for r in range(NY) for s in range(NC)]
    ).astype(jnp.int32)


def blocked_dot_kernel(depth, order, *refs):
    blocks, w, out = refs[:NH], refs[NH], refs[NH + 1]
    total = None
    for k in range(NH):
        start = pl.multiple_of(order[k] * depth, depth)
        part = jnp.dot(blocks[k][...], w[pl.ds(start, depth), :], preferred_element_type=F32)
        total = part if total is None else total + part
    out[...] = total.astype(out.dtype)


def blocked_dot(blocks, order, w, name):
    rows, depth = blocks[0].shape
    width = w.shape[1]
    vmem = pl.BlockSpec(memory_space=pltpu.VMEM)
    return pl.pallas_call(
        functools.partial(blocked_dot_kernel, depth),
        out_shape=jax.ShapeDtypeStruct((rows, width), BF),
        in_specs=[pl.BlockSpec(memory_space=pltpu.SMEM)] + [vmem] * (NH + 1),
        out_specs=vmem,
        compiler_params=pltpu.CompilerParams(vmem_limit_bytes=24 * 2**20),
        cost_estimate=pl.CostEstimate(
            flops=2 * rows * depth * NH * width,
            bytes_accessed=2 * (rows * depth * NH + depth * NH * width + rows * width),
            transcendentals=0,
        ),
        name=name,
    )(order, *blocks, w)


def z_shift(a, r):
    pairs = [(x * NZ + z, x * NZ + (z + r) % NZ) for x in range(NX) for z in range(NZ)]
    return lax.ppermute(a, "seq", pairs)


def x_shift(a, r):
    pairs = [(x * NZ + z, ((x + r) % NX) * NZ + z) for x in range(NX) for z in range(NZ)]
    return lax.ppermute(a, "seq", pairs)


def far_shift(a):
    pairs = []
    for x in range(NX):
        for z in range(NZ):
            for h in range(NH):
                step = 2 if h % NC else -2
                pairs.append(((x * NZ + z) * NH + h, (x * NZ + (z + step) % NZ) * NH + h))
    return lax.ppermute(a, ("seq", "head"), pairs)


def pick(copy_of, pos, value, slab, others):
    shard, row = value // STORE_DEV, value % STORE_DEV
    away = (shard % NZ - pos[1] + NZ) % NZ
    back = (pos[0] - shard // NZ + NX) % NX

    @pl.when(away == 0)
    def _():
        for r in range(NX):
            @pl.when(back == r)
            def _(r=r):
                copy_of(slab[r].at[row])

    for distances, source in others:
        hit = functools.reduce(jnp.logical_or, [away == d for d in distances])

        @pl.when(hit)
        def _(source=source):
            copy_of(source)


def first_kernel(pos, look, s0, s1, s2, s3, minus, plus, far, sems):
    slab = (s0, s1, s2, s3)
    jobs = [(1, minus, 0), (3, minus, SLOTS), (7, plus, 0), (5, plus, SLOTS), (4, far, 0)]
    for start in (True, False):
        for j, (k, out, base) in enumerate(jobs):
            for q in range(SLOTS):
                def move(source, out=out, i=base + q, sem=j * SLOTS + q):
                    copy = pltpu.make_async_copy(source, out.at[i], sems.at[sem])
                    copy.start() if start else copy.wait()

                pick(move, pos, look[k * SLOTS + q], slab, [])


def second_kernel(pos, look, s0, s1, s2, s3, minus_in, plus_in, far_in, minus, plus, sems):
    slab = (s0, s1, s2, s3)
    far_minus = jnp.where(pos[2] == 0, 2, -1)
    far_plus = jnp.where(pos[2] == 0, -1, 6)
    jobs = [(2, minus, minus_in, 1, far_minus), (6, plus, plus_in, 7, far_plus)]
    for start in (True, False):
        for j, (k, out, near, d, far_d) in enumerate(jobs):
            for q in range(SLOTS):
                def move(source, out=out, q=q, sem=j * SLOTS + q):
                    copy = pltpu.make_async_copy(source, out.at[q], sems.at[sem])
                    copy.start() if start else copy.wait()

                others = [((d,), near.at[SLOTS + q]), ((far_d,), far_in.at[q])]
                pick(move, pos, look[k * SLOTS + q], slab, others)


def slot_arrays(count, width):
    return jax.ShapeDtypeStruct((count, ROWS, width), BF)


def route(kernel, pos, look, arrays, counts, copies, name):
    width = arrays[0].shape[-1]
    return pl.pallas_call(
        kernel,
        out_shape=[slot_arrays(n, width) for n in counts],
        in_specs=[pl.BlockSpec(memory_space=pltpu.SMEM)] * 2
        + [pl.BlockSpec(memory_space=pl.ANY)] * len(arrays),
        out_specs=[pl.BlockSpec(memory_space=pl.ANY)] * len(counts),
        scratch_shapes=[pltpu.SemaphoreType.DMA((copies,))],
        cost_estimate=pl.CostEstimate(
            flops=0, bytes_accessed=4 * copies * ROWS * width, transcendentals=0
        ),
        name=name,
    )(pos, look, *arrays)


def encode_kernel(first, last, pos, order, look, *refs):
    slab, (minus_in, plus_in, minus2_in, plus2_in) = refs[:NX], refs[NX : NX + 4]
    ctx = refs[NX + 4 : NX + 4 + NH]
    out, nb, sems = refs[NX + 4 + NH :]
    width = nb.shape[-1]
    far_minus = jnp.where(pos[2] == 0, 4, -1)
    far_plus = jnp.where(pos[2] == 0, -1, 4)
    for start in (True, False):
        for q in range(SLOTS):
            def move(source, q=q):
                copy = pltpu.make_async_copy(source, nb.at[q], sems.at[q])
                copy.start() if start else copy.wait()

            others = [
                ((1,), minus_in.at[q]),
                ((7,), plus_in.at[q]),
                ((2, 3, far_minus), minus2_in.at[q]),
                ((5, 6, far_plus), plus2_in.at[q]),
            ]
            pick(move, pos, look[q], slab, others)
    heads = range(last - first)
    for r in range(NY):
        span = order[NC * r] // NC
        context = jnp.concatenate([ctx[NC * r][...], ctx[NC * r + 1][...]], axis=0)
        context = context[:, first * EHD : last * EHD]
        rows = nb[pl.ds(span * KN, KN)].reshape(KN * ROWS, width)
        scores = jnp.concatenate(
            [
                lax.dot_general(
                    rows[:, g * EHD : (g + 1) * EHD],
                    context[:, g * EHD : (g + 1) * EHD],
                    (((1,), (1,)), ((), ())),
                    preferred_element_type=F32,
                )
                for g in heads
            ],
            axis=0,
        ) * (1.0 / math.sqrt(EHD))
        weights = jnp.exp(scores - jnp.max(scores, axis=1, keepdims=True))
        weights = (weights / jnp.sum(weights, axis=1, keepdims=True)).astype(BF)
        mixed = jnp.concatenate(
            [
                jnp.dot(
                    weights[g * KN * ROWS : (g + 1) * KN * ROWS],
                    context[:, g * EHD : (g + 1) * EHD],
                    preferred_element_type=F32,
                )
                for g in heads
            ],
            axis=1,
        )
        encoded = (rows.astype(F32) + mixed).astype(BF)
        out[pl.ds(span * KN, KN)] = encoded.reshape(KN, ROWS, width)


def encode(chunk, pos, order, look, arrays, ctx_blocks):
    first, last = chunk
    width = (last - first) * EHD
    vmem = pl.BlockSpec(memory_space=pltpu.VMEM)
    smem = pl.BlockSpec(memory_space=pltpu.SMEM)
    return pl.pallas_call(
        functools.partial(encode_kernel, first, last),
        out_shape=slot_arrays(SLOTS, width),
        in_specs=[smem] * 3 + [pl.BlockSpec(memory_space=pl.ANY)] * len(arrays) + [vmem] * NH,
        out_specs=vmem,
        scratch_shapes=[
            pltpu.VMEM((SLOTS, ROWS, width), BF),
            pltpu.SemaphoreType.DMA((SLOTS,)),
        ],
        compiler_params=pltpu.CompilerParams(vmem_limit_bytes=24 * 2**20),
        cost_estimate=pl.CostEstimate(
            flops=4 * SLOTS * ROWS * CL * width,
            bytes_accessed=2 * 2 * SLOTS * ROWS * width + 2 * 256 * E,
            transcendentals=SLOTS * ROWS * CL * (last - first),
        ),
        name="encode",
    )(pos, order, look, *arrays, *ctx_blocks)


def attend_kernel(*refs):
    blocks = refs[: NH * len(CHUNKS)]
    q, wk, wv, out, rows, sems = refs[NH * len(CHUNKS) :]
    spans = rows.shape[0]
    copies = []
    for i, block in enumerate(blocks):
        first, last = CHUNKS[i // NH]
        place = rows.at[:, i % NH, :, pl.ds(first * EHD, (last - first) * EHD)]
        copies.append(pltpu.make_async_copy(block, place, sems.at[i]))
    for copy in copies:
        copy.start()
    for copy in copies:
        copy.wait()
    flat = rows[...].reshape(spans * KN * NL, E)
    keys = jnp.dot(flat, wk[...], preferred_element_type=F32).astype(BF)
    values = jnp.dot(flat, wv[...], preferred_element_type=F32).astype(BF)
    heads = q.shape[1] // HD
    span_rows = KN * NL
    units = [(s, h) for s in range(spans) for h in range(heads)]
    scores = jnp.concatenate(
        [
            lax.dot_general(
                q[s * CL : (s + 1) * CL, h * HD : (h + 1) * HD],
                keys[s * span_rows : (s + 1) * span_rows, h * HD : (h + 1) * HD],
                (((1,), (1,)), ((), ())),
                preferred_element_type=F32,
            )
            for s, h in units
        ],
        axis=0,
    ) * (1.0 / math.sqrt(HD))
    weights = jnp.exp(scores - jnp.max(scores, axis=1, keepdims=True))
    weights = (weights / jnp.sum(weights, axis=1, keepdims=True)).astype(BF)
    for i, (s, h) in enumerate(units):
        out[s * CL : (s + 1) * CL, h * HD : (h + 1) * HD] = jnp.dot(
            weights[i * CL : (i + 1) * CL],
            values[s * span_rows : (s + 1) * span_rows, h * HD : (h + 1) * HD],
            preferred_element_type=F32,
        ).astype(BF)


def attend(blocks, queries, key_weight, value_weight):
    tokens, width = queries.shape
    spans = tokens // CL
    vmem = pl.BlockSpec(memory_space=pltpu.VMEM)
    blocks = [b.reshape(spans, KN * ROWS, b.shape[-1]) for b in blocks]
    return pl.pallas_call(
        attend_kernel,
        out_shape=jax.ShapeDtypeStruct((tokens, width), BF),
        in_specs=[pl.BlockSpec(memory_space=pl.ANY)] * len(blocks) + [vmem] * 3,
        out_specs=vmem,
        scratch_shapes=[
            pltpu.VMEM((spans, NH, KN * ROWS, E), BF),
            pltpu.SemaphoreType.DMA((len(blocks),)),
        ],
        compiler_params=pltpu.CompilerParams(vmem_limit_bytes=32 * 2**20),
        cost_estimate=pl.CostEstimate(
            flops=4 * spans * KN * NL * E * width + 4 * tokens * KN * NL * width,
            bytes_accessed=2 * (spans * KN * NL * E + 2 * E * width + 2 * tokens * width),
            transcendentals=tokens * KN * NL * 2,
        ),
        name="attend",
    )(*blocks, queries, key_weight, value_weight)


def sum_context(partial, y, c):
    parts = partial.reshape(NY, NC, -1, E)
    mine = lax.dynamic_index_in_dim(parts, c, axis=1, keepdims=False)
    theirs = lax.dynamic_index_in_dim(parts, 1 - c, axis=1, keepdims=False)
    chip = mine + core_swap(theirs)
    total = lax.dynamic_index_in_dim(chip, y, axis=0, keepdims=False)
    for r in (1, 3, 2):
        sent = lax.dynamic_index_in_dim(chip, (y + r) % NY, axis=0, keepdims=False)
        total = total + y_shift(sent, r)
    return total.astype(BF)


def z_lists(look):
    lists = look.reshape(1, SLOTS)
    for r in (1, 2, 4):
        lists = jnp.concatenate([lists, z_shift(lists, r)], axis=0)
    return lists.reshape(NZ * SLOTS)


def fetch(chunk, store, pos, look, head):
    first, last = chunk
    own = lax.dynamic_slice(
        store,
        (0, head * ROWS, first * EHD),
        (STORE_DEV, ROWS, (last - first) * EHD),
    )
    slab = [own] + [x_shift(own, r) for r in (1, 3, 2)]
    slab = [slab[0], slab[1], slab[3], slab[2]]
    minus, plus, far = route(
        first_kernel, pos, look, slab, (2 * SLOTS, 2 * SLOTS, SLOTS), 5 * SLOTS, "first"
    )
    minus, plus, far = z_shift(minus, -1), z_shift(plus, 1), far_shift(far)
    minus2, plus2 = route(
        second_kernel, pos, look, slab + [minus, plus, far], (SLOTS, SLOTS), 2 * SLOTS, "second"
    )
    return slab + [minus, plus, z_shift(minus2, -2), z_shift(plus2, 2)]


def local(
    tokens,
    neighbour_shard,
    neighbour_row,
    store_rows,
    context_weight,
    query_weight,
    key_weight,
    value_weight,
    output_weight,
):
    head = lax.axis_index("head")
    y, c = head // NC, head % NC
    order = block_order(y, c)
    seq = lax.axis_index("seq")
    pos = jnp.stack([seq // NZ, seq % NZ, c]).astype(jnp.int32)
    look = z_lists((neighbour_shard * STORE_DEV + neighbour_row).reshape(SLOTS))
    fetched = [fetch(chunk, store_rows, pos, look, head) for chunk in CHUNKS]
    partial = jnp.dot(tokens, context_weight, preferred_element_type=F32)
    context = sum_context(partial, y, c)
    ctx_blocks = [b for pair in head_blocks(context) for b in pair]
    tok_blocks = [b for pair in head_blocks(tokens) for b in pair]
    queries = blocked_dot(tok_blocks, order, query_weight, "queries")
    enc_blocks = []
    for chunk, arrays in zip(CHUNKS, fetched):
        encoded = encode(chunk, pos, order, look, arrays, ctx_blocks)
        enc_blocks += [b for pair in head_blocks(encoded) for b in pair]
    attention = attend(enc_blocks, queries, key_weight, value_weight)
    att_blocks = [b for pair in head_blocks(attention) for b in pair]
    return blocked_dot(att_blocks, order, output_weight, "project")


def solution(mesh):
    placed = (
        P("seq", "head"),
        P("seq", None),
        P("seq", None),
        P("seq", None, None),
        P("head", None),
        P(None, "head"),
        P(None, "head"),
        P(None, "head"),
        P(None, "head"),
    )
    return jax.shard_map(
        local, mesh=mesh, in_specs=placed, out_specs=P("seq", "head"), check_vma=False
    )
```

```python
import functools
import math

import jax
import jax.numpy as jnp
from jax import lax
from jax.experimental import pallas as pl
from jax.experimental.pallas import tpu as pltpu
from jax.sharding import PartitionSpec as P

HD = 128
E = 896
CL = 64
NL = 128
KN = 2
EHD = 128
NX, NZ, NY, NC = 4, 8, 4, 2
NS = NX * NZ
NH = NY * NC
STORE_DEV = 16
SLOTS = 8
ROWS = NL // NH
PIECES = ((0, 512), (512, 896))
BF = jnp.bfloat16
F32 = jnp.float32

VMEM = pl.BlockSpec(memory_space=pltpu.VMEM)
SMEM = pl.BlockSpec(memory_space=pltpu.SMEM)
ANY = pl.BlockSpec(memory_space=pl.ANY)


def without(count, at, kernel, *refs):
    kernel(*refs[:at], *refs[at + count :])


def whole(body, arrays, outs, name, lists=(), after=(), scratch=(), limit=8):
    size = sum(a.size * a.dtype.itemsize for a in [*arrays, *outs])
    return pl.pallas_call(
        functools.partial(without, len(after), len(lists) + len(arrays), body),
        out_shape=outs,
        in_specs=[SMEM] * len(lists) + [VMEM] * len(arrays) + [ANY] * len(after),
        out_specs=[VMEM] * len(outs),
        scratch_shapes=scratch,
        compiler_params=pltpu.CompilerParams(vmem_limit_bytes=limit * 2**20),
        cost_estimate=pl.CostEstimate(flops=0, bytes_accessed=size, transcendentals=0),
        name=name,
    )(*lists, *arrays, *after)


def y_shift(a, r):
    pairs = [(y * NC + c, ((y + r) % NY) * NC + c) for y in range(NY) for c in range(NC)]
    return lax.ppermute(a, "head", pairs)


def core_swap(a):
    return lax.ppermute(a, "head", [(h, h ^ 1) for h in range(NH)])


def z_shift(a, r):
    pairs = [(x * NZ + z, x * NZ + (z + r) % NZ) for x in range(NX) for z in range(NZ)]
    return lax.ppermute(a, "seq", pairs)


def x_shift(a, r):
    pairs = [(x * NZ + z, ((x + r) % NX) * NZ + z) for x in range(NX) for z in range(NZ)]
    return lax.ppermute(a, "seq", pairs)


def far_shift(a):
    pairs = []
    for x in range(NX):
        for z in range(NZ):
            for h in range(NH):
                step = 2 if h % NC else -2
                pairs.append(((x * NZ + z) * NH + h, (x * NZ + (z + step) % NZ) * NH + h))
    return lax.ppermute(a, ("seq", "head"), pairs)


def chip_blocks(a):
    one, three, two = [y_shift(a, r) for r in (1, 3, 2)]
    return [a, one, two, three]


def chip_blocks_in_turn(a):
    one, three = y_shift(a, 1), y_shift(a, 3)
    return [a, one, y_shift(one, 1), three]


def with_swaps(blocks):
    return [b for own in blocks for b in (own, core_swap(own))]


def source_head(k):
    head = lax.axis_index("head")
    y, c = head // NC, head % NC
    return ((y - k // NC + NY) % NY) * NC + (c if k % NC == 0 else 1 - c)


def partial_kernel(tokens, weight, mine, theirs):
    c = lax.axis_index("head") % NC
    total = jnp.dot(tokens[...], weight[...], preferred_element_type=F32)
    parts = total.reshape(NY, NC, -1, E)
    mine[...] = jnp.where(c == 0, parts[:, 0], parts[:, 1])
    theirs[...] = jnp.where(c == 0, parts[:, 1], parts[:, 0])


def chip_sum_kernel(mine, received, *outs):
    y = lax.axis_index("head") // NC
    for r, out in enumerate(outs):
        to = (y + r) % NY
        out[...] = mine[to] + received[to]


def pack_kernel(one, two, three, four, tokens, out):
    rows = tokens.shape[0]
    part = one.shape[0]
    out[:rows] = tokens[...]
    context = (one[...] + two[...] + three[...] + four[...]).astype(BF)
    for i, (first, last) in enumerate(PIECES):
        start = rows + i * part
        out[start : start + part, : last - first] = context[:, first:last]


def packed_context(tokens, weight, after):
    rows, width = tokens.shape
    part = rows // NH
    half = jax.ShapeDtypeStruct((NY, part, E), F32)
    mine, theirs = whole(partial_kernel, [tokens, weight], [half, half], "partial", after=after)
    outs = [jax.ShapeDtypeStruct((part, E), F32)] * NY
    own, *sent = whole(chip_sum_kernel, [mine, core_swap(theirs)], outs, "chip_sum")
    received = [y_shift(sent[r - 1], r) for r in (1, 3, 2)]
    out = jax.ShapeDtypeStruct((rows + len(PIECES) * part, width), BF)
    return whole(pack_kernel, [own, *received, tokens], [out], "pack")[0]


def z_lists(lists, shifts):
    for r in shifts:
        lists = jnp.concatenate([lists, z_shift(lists, r)], axis=0)
    return lists


def slab_of(store):
    own = lax.dynamic_slice_in_dim(store, lax.axis_index("head") * ROWS, ROWS, axis=1)
    one, three, two = [x_shift(own, r) for r in (1, 3, 2)]
    return [own, one, two, three]


def locate(value):
    seq = lax.axis_index("seq")
    shard = value // STORE_DEV
    away = (shard % NZ - seq % NZ + NZ) % NZ
    back = (seq // NZ - shard // NZ + NX) % NX
    return away, back, value % STORE_DEV


def from_slab(slab, back, row):
    value = slab[0][row]
    for r in range(1, NX):
        value = jnp.where(back == r, slab[r][row], value)
    return value


def first_kernel(look, s0, s1, s2, s3, minus, plus, far):
    slab = (s0, s1, s2, s3)
    for k, out, base in [
        (1, minus, 0),
        (3, minus, SLOTS),
        (7, plus, 0),
        (5, plus, SLOTS),
        (4, far, 0),
    ]:
        for q in range(SLOTS):
            _, back, row = locate(look[k, q])
            out[base + q] = from_slab(slab, back, row)


def second_kernel(look, s0, s1, s2, s3, minus_in, plus_in, far_in, minus, plus, mine):
    slab = (s0, s1, s2, s3)
    for k, out, near, d in [(2, minus, minus_in, 1), (6, plus, plus_in, 7)]:
        for q in range(SLOTS):
            away, back, row = locate(look[k, q])
            value = jnp.where(away == d, near[SLOTS + q], far_in[q])
            out[q] = jnp.where(away == 0, from_slab(slab, back, row), value)
    for q in range(SLOTS):
        away, back, row = locate(look[0, q])
        value = jnp.where(away == 1, minus_in[q], plus_in[q])
        mine[q] = jnp.where(away == 0, from_slab(slab, back, row), value)


def slots(count):
    return jax.ShapeDtypeStruct((count, ROWS, E), BF)


def fetch(slab, look, before_first, before_second):
    outs = [slots(2 * SLOTS), slots(2 * SLOTS), slots(SLOTS)]
    minus, plus, far = whole(first_kernel, slab, outs, "first", [look], before_first)
    sent = [z_shift(minus, -1), z_shift(plus, 1), far_shift(far)]
    outs = [slots(SLOTS)] * 3
    minus, plus, mine = whole(second_kernel, slab + sent, outs, "second", [look], before_second)
    return [mine, z_shift(minus, -2), z_shift(plus, 2)]


def queries_kernel(*refs):
    blocks, w, (out, context) = refs[:NH], refs[NH], refs[NH + 1 :]
    rows = out.shape[0]
    part = context.shape[0] // NH
    depth = w.shape[0] // NH
    total = None
    for k in range(NH):
        start = pl.multiple_of(source_head(k) * depth, depth)
        dot = jnp.dot(blocks[k][:rows], w[pl.ds(start, depth), :], preferred_element_type=F32)
        total = dot if total is None else total + dot
        for i, (first, last) in enumerate(PIECES):
            at = rows + i * part
            context[k * part : (k + 1) * part, first:last] = blocks[k][at : at + part, : last - first]
    out[...] = total.astype(out.dtype)


def encode_kernel(look, mine, ahead_in, behind_in, ctx, out, nb):
    width = nb.shape[-1]
    part = ctx.shape[0] // NH
    core = lax.axis_index("head") % NC
    for q in range(SLOTS):
        away, _, _ = locate(look[0, q])
        ahead = (away == 2) | (away == 3) | ((away == 4) & (core == 0))
        near = (away == 0) | (away == 1) | (away == NZ - 1)
        nb[q] = jnp.where(near, mine[q], jnp.where(ahead, ahead_in[q], behind_in[q]))
    heads = range(width // EHD)
    for r in range(NY):
        span = source_head(NC * r) // NC
        context = ctx[NC * r * part : NC * (r + 1) * part]
        rows = nb[pl.ds(span * KN, KN)].reshape(KN * ROWS, width)
        scores = jnp.concatenate(
            [
                lax.dot_general(
                    rows[:, g * EHD : (g + 1) * EHD],
                    context[:, g * EHD : (g + 1) * EHD],
                    (((1,), (1,)), ((), ())),
                    preferred_element_type=F32,
                )
                for g in heads
            ],
            axis=0,
        ) * (1.0 / math.sqrt(EHD))
        weights = jnp.exp(scores - jnp.max(scores, axis=1, keepdims=True))
        weights = (weights / jnp.sum(weights, axis=1, keepdims=True)).astype(BF)
        mixed = jnp.concatenate(
            [
                jnp.dot(
                    weights[g * KN * ROWS : (g + 1) * KN * ROWS],
                    context[:, g * EHD : (g + 1) * EHD],
                    preferred_element_type=F32,
                )
                for g in heads
            ],
            axis=1,
        )
        encoded = (rows.astype(F32) + mixed).astype(BF)
        out[pl.ds(span * KN, KN)] = encoded.reshape(KN, ROWS, width)


def attend_kernel(*refs):
    blocks = refs[:NH]
    q_hbm, wk_hbm, wv_hbm, out, rows, q, wk, wv, sems = refs[NH:]
    spans = rows.shape[0]
    pairs = [(block, rows.at[:, k]) for k, block in enumerate(blocks)]
    pairs += [(wk_hbm, wk), (wv_hbm, wv), (q_hbm, q)]
    copies = [pltpu.make_async_copy(a, b, sems.at[i]) for i, (a, b) in enumerate(pairs)]
    for copy in copies:
        copy.start()
    for copy in copies:
        copy.wait()
    flat = rows[...].reshape(spans * KN * NL, E)
    keys = jnp.dot(flat, wk[...], preferred_element_type=F32).astype(BF)
    values = jnp.dot(flat, wv[...], preferred_element_type=F32).astype(BF)
    heads = q.shape[1] // HD
    span_rows = KN * NL
    units = [(s, h) for s in range(spans) for h in range(heads)]
    scores = jnp.concatenate(
        [
            lax.dot_general(
                q[s * CL : (s + 1) * CL, h * HD : (h + 1) * HD],
                keys[s * span_rows : (s + 1) * span_rows, h * HD : (h + 1) * HD],
                (((1,), (1,)), ((), ())),
                preferred_element_type=F32,
            )
            for s, h in units
        ],
        axis=0,
    ) * (1.0 / math.sqrt(HD))
    weights = jnp.exp(scores - jnp.max(scores, axis=1, keepdims=True))
    weights = (weights / jnp.sum(weights, axis=1, keepdims=True)).astype(BF)
    for i, (s, h) in enumerate(units):
        out[s * CL : (s + 1) * CL, h * HD : (h + 1) * HD] = jnp.dot(
            weights[i * CL : (i + 1) * CL],
            values[s * span_rows : (s + 1) * span_rows, h * HD : (h + 1) * HD],
            preferred_element_type=F32,
        ).astype(BF)


def attend(blocks, queries, key_weight, value_weight):
    tokens, width = queries.shape
    spans = tokens // CL
    blocks = [b.reshape(spans, KN * ROWS, E) for b in blocks]
    arrays = [queries, key_weight, value_weight]
    return pl.pallas_call(
        attend_kernel,
        out_shape=jax.ShapeDtypeStruct((tokens, width), BF),
        in_specs=[ANY] * (NH + 3),
        out_specs=VMEM,
        scratch_shapes=[
            pltpu.VMEM((spans, NH, KN * ROWS, E), BF),
            *[pltpu.VMEM(a.shape, BF) for a in arrays],
            pltpu.SemaphoreType.DMA((NH + 3,)),
        ],
        compiler_params=pltpu.CompilerParams(vmem_limit_bytes=14 * 2**20),
        cost_estimate=pl.CostEstimate(
            flops=4 * spans * KN * NL * E * width,
            bytes_accessed=2 * (spans * KN * NL * E + 2 * E * width + 2 * tokens * width),
            transcendentals=0,
        ),
        name="attend",
    )(*blocks, *arrays)


def project_kernel(*refs):
    blocks, w, out = refs[:NH], refs[NH], refs[NH + 1]
    depth = w.shape[0] // NH
    total = None
    for k in range(NH):
        start = pl.multiple_of(source_head(k) * depth, depth)
        dot = jnp.dot(blocks[k][...], w[pl.ds(start, depth), :], preferred_element_type=F32)
        total = dot if total is None else total + dot
    out[...] = total.astype(out.dtype)


def project(blocks, w):
    rows = blocks[0].shape[0]
    return pl.pallas_call(
        project_kernel,
        out_shape=jax.ShapeDtypeStruct((rows, w.shape[1]), BF),
        in_specs=[VMEM] * (NH + 1),
        out_specs=VMEM,
        compiler_params=pltpu.CompilerParams(vmem_limit_bytes=8 * 2**20),
        cost_estimate=pl.CostEstimate(
            flops=2 * rows * w.size, bytes_accessed=4 * w.size, transcendentals=0
        ),
        name="project",
    )(*blocks, w)


def local(
    tokens,
    neighbour_shard,
    neighbour_row,
    store_rows,
    context_weight,
    query_weight,
    key_weight,
    value_weight,
    output_weight,
):
    rows = tokens.shape[0]
    slab = slab_of(store_rows)
    own = (neighbour_shard * STORE_DEV + neighbour_row).reshape(1, SLOTS)
    look = z_lists(own, (1,))
    packed = packed_context(tokens, context_weight, [look])
    look = z_lists(look, (2, 4))
    chips = chip_blocks_in_turn(packed)
    fetched = fetch(slab, look, (), ())
    outs = [
        jax.ShapeDtypeStruct((rows, query_weight.shape[1]), BF),
        jax.ShapeDtypeStruct((rows, E), BF),
    ]
    queries, context = whole(
        queries_kernel, [*with_swaps(chips), query_weight], outs, "queries"
    )
    scratch = [pltpu.VMEM((SLOTS, ROWS, E), BF)]
    encoded = whole(
        encode_kernel, [*fetched, context], [slots(SLOTS)], "encode", [look], scratch=scratch
    )[0]
    attention = attend(with_swaps(chip_blocks(encoded)), queries, key_weight, value_weight)
    return project(with_swaps(chip_blocks(attention)), output_weight)


def solution(mesh):
    placed = (
        P("seq", "head"),
        P("seq", None),
        P("seq", None),
        P("seq", None, None),
        P("head", None),
        P(None, "head"),
        P(None, "head"),
        P(None, "head"),
        P(None, "head"),
    )
    return jax.shard_map(
        local, mesh=mesh, in_specs=placed, out_specs=P("seq", "head"), check_vma=False
    )
```

```python
import functools
import math

import jax
import jax.numpy as jnp
from jax import lax
from jax.experimental import pallas as pl
from jax.experimental.pallas import tpu as pltpu
from jax.sharding import PartitionSpec as P

HD = 128
E = 896
CL = 64
NL = 128
KN = 2
EHD = 128
NX, NZ, NY, NC = 4, 8, 4, 2
NS = NX * NZ
NH = NY * NC
STORE_DEV = 16
SLOTS = 8
ROWS = NL // NH
PIECES = ((0, 512), (512, 896))
BF = jnp.bfloat16
F32 = jnp.float32

VMEM = pl.BlockSpec(memory_space=pltpu.VMEM)
SMEM = pl.BlockSpec(memory_space=pltpu.SMEM)
ANY = pl.BlockSpec(memory_space=pl.ANY)


def without(count, at, kernel, *refs):
    kernel(*refs[:at], *refs[at + count :])


def whole(body, arrays, outs, name, lists=(), after=(), scratch=(), limit=8):
    size = sum(a.size * a.dtype.itemsize for a in [*arrays, *outs])
    return pl.pallas_call(
        functools.partial(without, len(after), len(lists) + len(arrays), body),
        out_shape=outs,
        in_specs=[SMEM] * len(lists) + [VMEM] * len(arrays) + [ANY] * len(after),
        out_specs=[VMEM] * len(outs),
        scratch_shapes=scratch,
        compiler_params=pltpu.CompilerParams(vmem_limit_bytes=limit * 2**20),
        cost_estimate=pl.CostEstimate(flops=0, bytes_accessed=size, transcendentals=0),
        name=name,
    )(*lists, *arrays, *after)


def y_shift(a, r):
    pairs = [(y * NC + c, ((y + r) % NY) * NC + c) for y in range(NY) for c in range(NC)]
    return lax.ppermute(a, "head", pairs)


def core_swap(a):
    return lax.ppermute(a, "head", [(h, h ^ 1) for h in range(NH)])


def z_shift(a, r):
    pairs = [(x * NZ + z, x * NZ + (z + r) % NZ) for x in range(NX) for z in range(NZ)]
    return lax.ppermute(a, "seq", pairs)


def x_shift(a, r):
    pairs = [(x * NZ + z, ((x + r) % NX) * NZ + z) for x in range(NX) for z in range(NZ)]
    return lax.ppermute(a, "seq", pairs)


def far_shift(a):
    pairs = []
    for x in range(NX):
        for z in range(NZ):
            for h in range(NH):
                step = 2 if h % NC else -2
                pairs.append(((x * NZ + z) * NH + h, (x * NZ + (z + step) % NZ) * NH + h))
    return lax.ppermute(a, ("seq", "head"), pairs)


def chip_blocks(a):
    one, three, two = [y_shift(a, r) for r in (1, 3, 2)]
    return [a, one, two, three]


def chip_blocks_in_turn(a):
    one, three = y_shift(a, 1), y_shift(a, 3)
    return [a, one, y_shift(one, 1), three]


def with_swaps(blocks):
    return [b for own in blocks for b in (own, core_swap(own))]


def source_head(k):
    head = lax.axis_index("head")
    y, c = head // NC, head % NC
    return ((y - k // NC + NY) % NY) * NC + (c if k % NC == 0 else 1 - c)


def partial_kernel(tokens, weight, mine, theirs):
    c = lax.axis_index("head") % NC
    total = jnp.dot(tokens[...], weight[...], preferred_element_type=F32)
    parts = total.reshape(NY, NC, -1, E)
    mine[...] = jnp.where(c == 0, parts[:, 0], parts[:, 1])
    theirs[...] = jnp.where(c == 0, parts[:, 1], parts[:, 0])


def chip_sum_kernel(mine, received, *outs):
    y = lax.axis_index("head") // NC
    for r, out in enumerate(outs):
        to = (y + r) % NY
        out[...] = mine[to] + received[to]


def pack_kernel(one, two, three, four, tokens, out):
    rows = tokens.shape[0]
    part = one.shape[0]
    out[:rows] = tokens[...]
    context = (one[...] + two[...] + three[...] + four[...]).astype(BF)
    for i, (first, last) in enumerate(PIECES):
        start = rows + i * part
        out[start : start + part, : last - first] = context[:, first:last]


def half_sums(tokens, weight, y, c):
    rows = tokens.shape[0]
    part = rows // NH
    parts = jnp.dot(tokens, weight, preferred_element_type=F32).reshape(NY, NC, part, E)
    mine = lax.dynamic_index_in_dim(parts, c, axis=1, keepdims=False)
    theirs = lax.dynamic_index_in_dim(parts, 1 - c, axis=1, keepdims=False)
    return mine, core_swap(theirs)


def packed_context(halves, tokens, after, after_sum):
    rows, width = tokens.shape
    part = rows // NH
    outs = [jax.ShapeDtypeStruct((part, E), F32)] * NY
    own, *sent = whole(chip_sum_kernel, list(halves), outs, "chip_sum", after=after)
    received = [y_shift(sent[r - 1], r) for r in (1, 3, 2)]
    out = jax.ShapeDtypeStruct((rows + len(PIECES) * part, width), BF)
    return whole(pack_kernel, [own, *received, tokens], [out], "pack", after=after_sum)[0]


def z_lists(lists, shifts):
    for r in shifts:
        lists = jnp.concatenate([lists, z_shift(lists, r)], axis=0)
    return lists


def slab_of(store):
    own = lax.dynamic_slice_in_dim(store, lax.axis_index("head") * ROWS, ROWS, axis=1)
    one, three, two = [x_shift(own, r) for r in (1, 3, 2)]
    return [own, one, two, three]


def locate(value):
    seq = lax.axis_index("seq")
    shard = value // STORE_DEV
    away = (shard % NZ - seq % NZ + NZ) % NZ
    back = (seq // NZ - shard // NZ + NX) % NX
    return away, back, value % STORE_DEV


def from_slab(slab, back, row):
    value = slab[0][row]
    for r in range(1, NX):
        value = jnp.where(back == r, slab[r][row], value)
    return value


def first_kernel(look, s0, s1, s2, s3, minus, plus, far):
    slab = (s0, s1, s2, s3)
    for k, out, base in [
        (1, minus, 0),
        (3, minus, SLOTS),
        (7, plus, 0),
        (5, plus, SLOTS),
        (4, far, 0),
    ]:
        for q in range(SLOTS):
            _, back, row = locate(look[k, q])
            out[base + q] = from_slab(slab, back, row)


def second_kernel(look, s0, s1, s2, s3, minus_in, plus_in, far_in, minus, plus, mine):
    slab = (s0, s1, s2, s3)
    for k, out, near, d in [(2, minus, minus_in, 1), (6, plus, plus_in, 7)]:
        for q in range(SLOTS):
            away, back, row = locate(look[k, q])
            value = jnp.where(away == d, near[SLOTS + q], far_in[q])
            out[q] = jnp.where(away == 0, from_slab(slab, back, row), value)
    for q in range(SLOTS):
        away, back, row = locate(look[0, q])
        value = jnp.where(away == 1, minus_in[q], plus_in[q])
        mine[q] = jnp.where(away == 0, from_slab(slab, back, row), value)


def slots(count):
    return jax.ShapeDtypeStruct((count, ROWS, E), BF)


def first_hop(slab, look):
    outs = [slots(2 * SLOTS), slots(2 * SLOTS), slots(SLOTS)]
    return whole(first_kernel, slab, outs, "first", [look])


def sent_on(slots_out):
    minus, plus, far = slots_out
    return [z_shift(minus, -1), z_shift(plus, 1), far_shift(far)]


def second_hop(slab, look, arrays):
    return whole(second_kernel, slab + arrays, [slots(SLOTS)] * 3, "second", [look])


def stack_kernel(*refs):
    *blocks, out = refs
    for r, block in enumerate(blocks):
        out[r] = block[...]


def queries_kernel(own, other, w, out, context):
    blocks = [(own, other)[k % NC].at[k // NC] for k in range(NH)]
    rows = out.shape[0]
    part = context.shape[0] // NH
    depth = w.shape[0] // NH
    total = None
    for k in range(NH):
        start = pl.multiple_of(source_head(k) * depth, depth)
        dot = jnp.dot(blocks[k][:rows], w[pl.ds(start, depth), :], preferred_element_type=F32)
        total = dot if total is None else total + dot
        for i, (first, last) in enumerate(PIECES):
            at = rows + i * part
            context[k * part : (k + 1) * part, first:last] = blocks[k][at : at + part, : last - first]
    out[...] = total.astype(out.dtype)


def encode_kernel(look, mine, ahead_in, behind_in, ctx, out, nb):
    width = nb.shape[-1]
    part = ctx.shape[0] // NH
    core = lax.axis_index("head") % NC
    for q in range(SLOTS):
        away, _, _ = locate(look[0, q])
        ahead = (away == 2) | (away == 3) | ((away == 4) & (core == 0))
        near = (away == 0) | (away == 1) | (away == NZ - 1)
        nb[q] = jnp.where(near, mine[q], jnp.where(ahead, ahead_in[q], behind_in[q]))
    heads = range(width // EHD)
    for r in range(NY):
        span = source_head(NC * r) // NC
        context = ctx[NC * r * part : NC * (r + 1) * part]
        rows = nb[pl.ds(span * KN, KN)].reshape(KN * ROWS, width)
        scores = jnp.concatenate(
            [
                lax.dot_general(
                    rows[:, g * EHD : (g + 1) * EHD],
                    context[:, g * EHD : (g + 1) * EHD],
                    (((1,), (1,)), ((), ())),
                    preferred_element_type=F32,
                )
                for g in heads
            ],
            axis=0,
        ) * (1.0 / math.sqrt(EHD))
        weights = jnp.exp(scores - jnp.max(scores, axis=1, keepdims=True))
        weights = (weights / jnp.sum(weights, axis=1, keepdims=True)).astype(BF)
        mixed = jnp.concatenate(
            [
                jnp.dot(
                    weights[g * KN * ROWS : (g + 1) * KN * ROWS],
                    context[:, g * EHD : (g + 1) * EHD],
                    preferred_element_type=F32,
                )
                for g in heads
            ],
            axis=1,
        )
        encoded = (rows.astype(F32) + mixed).astype(BF)
        out[pl.ds(span * KN, KN)] = encoded.reshape(KN, ROWS, width)


def attend_kernel(*refs):
    blocks = refs[:NH]
    q_hbm, wk_hbm, wv_hbm, out, rows, q, wk, wv, sems = refs[NH:]
    spans = rows.shape[0]
    pairs = [(block, rows.at[:, k]) for k, block in enumerate(blocks)]
    pairs += [(wk_hbm, wk), (wv_hbm, wv), (q_hbm, q)]
    copies = [pltpu.make_async_copy(a, b, sems.at[i]) for i, (a, b) in enumerate(pairs)]
    for copy in copies:
        copy.start()
    for copy in copies:
        copy.wait()
    flat = rows[...].reshape(spans * KN * NL, E)
    keys = jnp.dot(flat, wk[...], preferred_element_type=F32).astype(BF)
    values = jnp.dot(flat, wv[...], preferred_element_type=F32).astype(BF)
    heads = q.shape[1] // HD
    span_rows = KN * NL
    units = [(s, h) for s in range(spans) for h in range(heads)]
    scores = jnp.concatenate(
        [
            lax.dot_general(
                q[s * CL : (s + 1) * CL, h * HD : (h + 1) * HD],
                keys[s * span_rows : (s + 1) * span_rows, h * HD : (h + 1) * HD],
                (((1,), (1,)), ((), ())),
                preferred_element_type=F32,
            )
            for s, h in units
        ],
        axis=0,
    ) * (1.0 / math.sqrt(HD))
    weights = jnp.exp(scores - jnp.max(scores, axis=1, keepdims=True))
    weights = (weights / jnp.sum(weights, axis=1, keepdims=True)).astype(BF)
    for i, (s, h) in enumerate(units):
        out[s * CL : (s + 1) * CL, h * HD : (h + 1) * HD] = jnp.dot(
            weights[i * CL : (i + 1) * CL],
            values[s * span_rows : (s + 1) * span_rows, h * HD : (h + 1) * HD],
            preferred_element_type=F32,
        ).astype(BF)


def attend(blocks, queries, key_weight, value_weight):
    tokens, width = queries.shape
    spans = tokens // CL
    blocks = [b.reshape(spans, KN * ROWS, E) for b in blocks]
    arrays = [queries, key_weight, value_weight]
    return pl.pallas_call(
        attend_kernel,
        out_shape=jax.ShapeDtypeStruct((tokens, width), BF),
        in_specs=[ANY] * (NH + 3),
        out_specs=VMEM,
        scratch_shapes=[
            pltpu.VMEM((spans, NH, KN * ROWS, E), BF),
            *[pltpu.VMEM(a.shape, BF) for a in arrays],
            pltpu.SemaphoreType.DMA((NH + 3,)),
        ],
        compiler_params=pltpu.CompilerParams(vmem_limit_bytes=14 * 2**20),
        cost_estimate=pl.CostEstimate(
            flops=4 * spans * KN * NL * E * width,
            bytes_accessed=2 * (spans * KN * NL * E + 2 * E * width + 2 * tokens * width),
            transcendentals=0,
        ),
        name="attend",
    )(*blocks, *arrays)


def project_kernel(*refs):
    blocks, w, out = refs[:NH], refs[NH], refs[NH + 1]
    depth = w.shape[0] // NH
    total = None
    for k in range(NH):
        start = pl.multiple_of(source_head(k) * depth, depth)
        dot = jnp.dot(blocks[k][...], w[pl.ds(start, depth), :], preferred_element_type=F32)
        total = dot if total is None else total + dot
    out[...] = total.astype(out.dtype)


def project(blocks, w):
    rows = blocks[0].shape[0]
    return pl.pallas_call(
        project_kernel,
        out_shape=jax.ShapeDtypeStruct((rows, w.shape[1]), BF),
        in_specs=[VMEM] * (NH + 1),
        out_specs=VMEM,
        compiler_params=pltpu.CompilerParams(vmem_limit_bytes=8 * 2**20),
        cost_estimate=pl.CostEstimate(
            flops=2 * rows * w.size, bytes_accessed=4 * w.size, transcendentals=0
        ),
        name="project",
    )(*blocks, w)


def local(
    tokens,
    neighbour_shard,
    neighbour_row,
    store_rows,
    context_weight,
    query_weight,
    key_weight,
    value_weight,
    output_weight,
):
    rows = tokens.shape[0]
    head = lax.axis_index("head")
    slab = slab_of(store_rows)
    own = (neighbour_shard * STORE_DEV + neighbour_row).reshape(1, SLOTS)
    look = z_lists(own, (1, 2, 4))
    halves = half_sums(tokens, context_weight, head // NC, head % NC)
    sent = first_hop(slab, look)
    arrays = sent_on(sent)
    minus, plus, mine = second_hop(slab, look, arrays)
    fetched = [mine, z_shift(minus, -2), z_shift(plus, 2)]
    packed = packed_context(halves, tokens, (), arrays[:2])
    chips = chip_blocks(packed)
    outs = [jax.ShapeDtypeStruct((NY, *packed.shape), BF)]
    stacked = whole(stack_kernel, chips, outs, "stack", after=fetched[1:])[0]
    outs = [
        jax.ShapeDtypeStruct((rows, query_weight.shape[1]), BF),
        jax.ShapeDtypeStruct((rows, E), BF),
    ]
    queries, context = whole(
        queries_kernel, [stacked, core_swap(stacked), query_weight], outs, "queries"
    )
    scratch = [pltpu.VMEM((SLOTS, ROWS, E), BF)]
    encoded = whole(
        encode_kernel, [*fetched, context], [slots(SLOTS)], "encode", [look], scratch=scratch
    )[0]
    attention = attend(with_swaps(chip_blocks(encoded)), queries, key_weight, value_weight)
    return project(with_swaps(chip_blocks(attention)), output_weight)


def solution(mesh):
    placed = (
        P("seq", "head"),
        P("seq", None),
        P("seq", None),
        P("seq", None, None),
        P("head", None),
        P(None, "head"),
        P(None, "head"),
        P(None, "head"),
        P(None, "head"),
    )
    return jax.shard_map(
        local, mesh=mesh, in_specs=placed, out_specs=P("seq", "head"), check_vma=False
    )
```

```python
import functools
import math

import jax
import jax.numpy as jnp
from jax import lax
from jax.experimental import pallas as pl
from jax.experimental.pallas import tpu as pltpu
from jax.sharding import PartitionSpec as P

HD = 128
E = 896
CL = 64
NL = 128
KN = 2
EHD = 128
NX, NZ, NY, NC = 4, 8, 4, 2
NS = NX * NZ
NH = NY * NC
STORE_DEV = 16
SLOTS = 8
ROWS = NL // NH
PIECES = ((0, 512), (512, 896))
BF = jnp.bfloat16
F32 = jnp.float32

VMEM = pl.BlockSpec(memory_space=pltpu.VMEM)
SMEM = pl.BlockSpec(memory_space=pltpu.SMEM)
ANY = pl.BlockSpec(memory_space=pl.ANY)


def without(count, at, kernel, *refs):
    kernel(*refs[:at], *refs[at + count :])


def whole(body, arrays, outs, name, lists=(), after=(), scratch=(), limit=8):
    size = sum(a.size * a.dtype.itemsize for a in [*arrays, *outs])
    return pl.pallas_call(
        functools.partial(without, len(after), len(lists) + len(arrays), body),
        out_shape=outs,
        in_specs=[SMEM] * len(lists) + [VMEM] * len(arrays) + [ANY] * len(after),
        out_specs=[VMEM] * len(outs),
        scratch_shapes=scratch,
        compiler_params=pltpu.CompilerParams(vmem_limit_bytes=limit * 2**20),
        cost_estimate=pl.CostEstimate(flops=0, bytes_accessed=size, transcendentals=0),
        name=name,
    )(*lists, *arrays, *after)


def y_shift(a, r):
    pairs = [(y * NC + c, ((y + r) % NY) * NC + c) for y in range(NY) for c in range(NC)]
    return lax.ppermute(a, "head", pairs)


def core_swap(a):
    return lax.ppermute(a, "head", [(h, h ^ 1) for h in range(NH)])


def z_shift(a, r):
    pairs = [(x * NZ + z, x * NZ + (z + r) % NZ) for x in range(NX) for z in range(NZ)]
    return lax.ppermute(a, "seq", pairs)


def x_shift(a, r):
    pairs = [(x * NZ + z, ((x + r) % NX) * NZ + z) for x in range(NX) for z in range(NZ)]
    return lax.ppermute(a, "seq", pairs)


def far_shift(a):
    pairs = []
    for x in range(NX):
        for z in range(NZ):
            for h in range(NH):
                step = 2 if h % NC else -2
                pairs.append(((x * NZ + z) * NH + h, (x * NZ + (z + step) % NZ) * NH + h))
    return lax.ppermute(a, ("seq", "head"), pairs)


def chip_blocks(a):
    one, three, two = [y_shift(a, r) for r in (1, 3, 2)]
    return [a, one, two, three]


def chip_blocks_in_turn(a):
    one, three = y_shift(a, 1), y_shift(a, 3)
    return [a, one, y_shift(one, 1), three]


def with_swaps(blocks):
    return [b for own in blocks for b in (own, core_swap(own))]


def source_head(k):
    head = lax.axis_index("head")
    y, c = head // NC, head % NC
    return ((y - k // NC + NY) % NY) * NC + (c if k % NC == 0 else 1 - c)


def partial_kernel(tokens, weight, mine, theirs):
    c = lax.axis_index("head") % NC
    total = jnp.dot(tokens[...], weight[...], preferred_element_type=F32)
    parts = total.reshape(NY, NC, -1, E)
    mine[...] = jnp.where(c == 0, parts[:, 0], parts[:, 1])
    theirs[...] = jnp.where(c == 0, parts[:, 1], parts[:, 0])


def chip_sum_kernel(mine, received, *outs):
    y = lax.axis_index("head") // NC
    for r, out in enumerate(outs):
        to = (y + r) % NY
        out[...] = mine[to] + received[to]


def pack_kernel(one, two, three, four, tokens, out):
    rows = tokens.shape[0]
    part = one.shape[0]
    out[:rows] = tokens[...]
    context = (one[...] + two[...] + three[...] + four[...]).astype(BF)
    for i, (first, last) in enumerate(PIECES):
        start = rows + i * part
        out[start : start + part, : last - first] = context[:, first:last]


def half_sums(tokens, weight, y, c):
    rows = tokens.shape[0]
    part = rows // NH
    parts = jnp.dot(tokens, weight, preferred_element_type=F32).reshape(NY, NC, part, E)
    mine = lax.dynamic_index_in_dim(parts, c, axis=1, keepdims=False)
    theirs = lax.dynamic_index_in_dim(parts, 1 - c, axis=1, keepdims=False)
    return mine, core_swap(theirs)


def packed_context(halves, tokens, after, after_sum):
    rows, width = tokens.shape
    part = rows // NH
    outs = [jax.ShapeDtypeStruct((part, E), F32)] * NY
    own, *sent = whole(chip_sum_kernel, list(halves), outs, "chip_sum", after=after)
    received = [y_shift(sent[r - 1], r) for r in (1, 3, 2)]
    out = jax.ShapeDtypeStruct((rows + len(PIECES) * part, width), BF)
    return whole(pack_kernel, [own, *received, tokens], [out], "pack", after=after_sum)[0]


def z_lists(lists, shifts):
    for r in shifts:
        lists = jnp.concatenate([lists, z_shift(lists, r)], axis=0)
    return lists


def slab_of(store):
    own = lax.dynamic_slice_in_dim(store, lax.axis_index("head") * ROWS, ROWS, axis=1)
    one, three, two = [x_shift(own, r) for r in (1, 3, 2)]
    return [own, one, two, three]


def locate(value):
    seq = lax.axis_index("seq")
    shard = value // STORE_DEV
    away = (shard % NZ - seq % NZ + NZ) % NZ
    back = (seq // NZ - shard // NZ + NX) % NX
    return away, back, value % STORE_DEV


def from_slab(slab, back, row):
    value = slab[0][row]
    for r in range(1, NX):
        value = jnp.where(back == r, slab[r][row], value)
    return value


def first_kernel(look, s0, s1, s2, s3, minus, plus, far):
    slab = (s0, s1, s2, s3)
    for k, out, base in [
        (1, minus, 0),
        (3, minus, SLOTS),
        (7, plus, 0),
        (5, plus, SLOTS),
        (4, far, 0),
    ]:
        for q in range(SLOTS):
            _, back, row = locate(look[k, q])
            out[base + q] = from_slab(slab, back, row)


def second_kernel(look, s0, s1, s2, s3, minus_in, plus_in, far_in, minus, plus, mine):
    slab = (s0, s1, s2, s3)
    for k, out, near, d in [(2, minus, minus_in, 1), (6, plus, plus_in, 7)]:
        for q in range(SLOTS):
            away, back, row = locate(look[k, q])
            value = jnp.where(away == d, near[SLOTS + q], far_in[q])
            out[q] = jnp.where(away == 0, from_slab(slab, back, row), value)
    for q in range(SLOTS):
        away, back, row = locate(look[0, q])
        value = jnp.where(away == 1, minus_in[q], plus_in[q])
        mine[q] = jnp.where(away == 0, from_slab(slab, back, row), value)


def slots(count):
    return jax.ShapeDtypeStruct((count, ROWS, E), BF)


def first_hop(slab, look):
    outs = [slots(2 * SLOTS), slots(2 * SLOTS), slots(SLOTS)]
    return whole(first_kernel, slab, outs, "first", [look])


def sent_on(slots_out):
    minus, plus, far = slots_out
    return [z_shift(minus, -1), z_shift(plus, 1), far_shift(far)]


def second_hop(slab, look, arrays):
    return whole(second_kernel, slab + arrays, [slots(SLOTS)] * 3, "second", [look])


def stack_kernel(*refs):
    blocks, (tokens, context) = refs[:NY], refs[NY:]
    rows, part = tokens.shape[1], context.shape[1]
    for r, block in enumerate(blocks):
        tokens[r] = block[:rows]
        for i, (first, last) in enumerate(PIECES):
            at = rows + i * part
            context[r, :, first:last] = block[at : at + part, : last - first]


def queries_kernel(own, other, w, out):
    blocks = [(own, other)[k % NC].at[k // NC] for k in range(NH)]
    depth = w.shape[0] // NH
    total = None
    for k in range(NH):
        start = pl.multiple_of(source_head(k) * depth, depth)
        dot = jnp.dot(blocks[k][...], w[pl.ds(start, depth), :], preferred_element_type=F32)
        total = dot if total is None else total + dot
    out[...] = total.astype(out.dtype)


def encode_kernel(look, mine, ahead_in, behind_in, ctx, other_ctx, out, nb):
    width = nb.shape[-1]
    core = lax.axis_index("head") % NC
    for q in range(SLOTS):
        away, _, _ = locate(look[0, q])
        ahead = (away == 2) | (away == 3) | ((away == 4) & (core == 0))
        near = (away == 0) | (away == 1) | (away == NZ - 1)
        nb[q] = jnp.where(near, mine[q], jnp.where(ahead, ahead_in[q], behind_in[q]))
    heads = range(width // EHD)
    for r in range(NY):
        span = source_head(NC * r) // NC
        context = jnp.concatenate([ctx[r], other_ctx[r]], axis=0)
        rows = nb[pl.ds(span * KN, KN)].reshape(KN * ROWS, width)
        scores = jnp.concatenate(
            [
                lax.dot_general(
                    rows[:, g * EHD : (g + 1) * EHD],
                    context[:, g * EHD : (g + 1) * EHD],
                    (((1,), (1,)), ((), ())),
                    preferred_element_type=F32,
                )
                for g in heads
            ],
            axis=0,
        ) * (1.0 / math.sqrt(EHD))
        weights = jnp.exp(scores - jnp.max(scores, axis=1, keepdims=True))
        weights = (weights / jnp.sum(weights, axis=1, keepdims=True)).astype(BF)
        mixed = jnp.concatenate(
            [
                jnp.dot(
                    weights[g * KN * ROWS : (g + 1) * KN * ROWS],
                    context[:, g * EHD : (g + 1) * EHD],
                    preferred_element_type=F32,
                )
                for g in heads
            ],
            axis=1,
        )
        encoded = (rows.astype(F32) + mixed).astype(BF)
        out[pl.ds(span * KN, KN)] = encoded.reshape(KN, ROWS, width)


def attend_kernel(*refs):
    blocks = refs[:NH]
    q_hbm, wk_hbm, wv_hbm, out, rows, q, wk, wv, sems = refs[NH:]
    spans = rows.shape[0]
    pairs = [(block, rows.at[:, k]) for k, block in enumerate(blocks)]
    pairs += [(wk_hbm, wk), (wv_hbm, wv), (q_hbm, q)]
    copies = [pltpu.make_async_copy(a, b, sems.at[i]) for i, (a, b) in enumerate(pairs)]
    for copy in copies:
        copy.start()
    for copy in copies:
        copy.wait()
    flat = rows[...].reshape(spans * KN * NL, E)
    keys = jnp.dot(flat, wk[...], preferred_element_type=F32).astype(BF)
    values = jnp.dot(flat, wv[...], preferred_element_type=F32).astype(BF)
    heads = q.shape[1] // HD
    span_rows = KN * NL
    units = [(s, h) for s in range(spans) for h in range(heads)]
    scores = jnp.concatenate(
        [
            lax.dot_general(
                q[s * CL : (s + 1) * CL, h * HD : (h + 1) * HD],
                keys[s * span_rows : (s + 1) * span_rows, h * HD : (h + 1) * HD],
                (((1,), (1,)), ((), ())),
                preferred_element_type=F32,
            )
            for s, h in units
        ],
        axis=0,
    ) * (1.0 / math.sqrt(HD))
    weights = jnp.exp(scores - jnp.max(scores, axis=1, keepdims=True))
    weights = (weights / jnp.sum(weights, axis=1, keepdims=True)).astype(BF)
    for i, (s, h) in enumerate(units):
        out[s * CL : (s + 1) * CL, h * HD : (h + 1) * HD] = jnp.dot(
            weights[i * CL : (i + 1) * CL],
            values[s * span_rows : (s + 1) * span_rows, h * HD : (h + 1) * HD],
            preferred_element_type=F32,
        ).astype(BF)


def attend(blocks, queries, key_weight, value_weight):
    tokens, width = queries.shape
    spans = tokens // CL
    blocks = [b.reshape(spans, KN * ROWS, E) for b in blocks]
    arrays = [queries, key_weight, value_weight]
    return pl.pallas_call(
        attend_kernel,
        out_shape=jax.ShapeDtypeStruct((tokens, width), BF),
        in_specs=[ANY] * (NH + 3),
        out_specs=VMEM,
        scratch_shapes=[
            pltpu.VMEM((spans, NH, KN * ROWS, E), BF),
            *[pltpu.VMEM(a.shape, BF) for a in arrays],
            pltpu.SemaphoreType.DMA((NH + 3,)),
        ],
        compiler_params=pltpu.CompilerParams(vmem_limit_bytes=14 * 2**20),
        cost_estimate=pl.CostEstimate(
            flops=4 * spans * KN * NL * E * width,
            bytes_accessed=2 * (spans * KN * NL * E + 2 * E * width + 2 * tokens * width),
            transcendentals=0,
        ),
        name="attend",
    )(*blocks, *arrays)


def project_kernel(*refs):
    blocks, w, out = refs[:NH], refs[NH], refs[NH + 1]
    depth = w.shape[0] // NH
    total = None
    for k in range(NH):
        start = pl.multiple_of(source_head(k) * depth, depth)
        dot = jnp.dot(blocks[k][...], w[pl.ds(start, depth), :], preferred_element_type=F32)
        total = dot if total is None else total + dot
    out[...] = total.astype(out.dtype)


def project(blocks, w):
    rows = blocks[0].shape[0]
    return pl.pallas_call(
        project_kernel,
        out_shape=jax.ShapeDtypeStruct((rows, w.shape[1]), BF),
        in_specs=[VMEM] * (NH + 1),
        out_specs=VMEM,
        compiler_params=pltpu.CompilerParams(vmem_limit_bytes=8 * 2**20),
        cost_estimate=pl.CostEstimate(
            flops=2 * rows * w.size, bytes_accessed=4 * w.size, transcendentals=0
        ),
        name="project",
    )(*blocks, w)


def local(
    tokens,
    neighbour_shard,
    neighbour_row,
    store_rows,
    context_weight,
    query_weight,
    key_weight,
    value_weight,
    output_weight,
):
    rows = tokens.shape[0]
    head = lax.axis_index("head")
    slab = slab_of(store_rows)
    own = (neighbour_shard * STORE_DEV + neighbour_row).reshape(1, SLOTS)
    look = z_lists(own, (1, 2, 4))
    halves = half_sums(tokens, context_weight, head // NC, head % NC)
    sent = first_hop(slab, look)
    arrays = sent_on(sent)
    minus, plus, mine = second_hop(slab, look, arrays)
    fetched = [mine, z_shift(minus, -2), z_shift(plus, 2)]
    packed = packed_context(halves, tokens, (), arrays[:2])
    chips = chip_blocks(packed)
    outs = [
        jax.ShapeDtypeStruct((NY, *tokens.shape), BF),
        jax.ShapeDtypeStruct((NY, rows // NH, E), BF),
    ]
    tok_stack, context = whole(stack_kernel, chips, outs, "stack", after=fetched[1:])
    scratch = [pltpu.VMEM((SLOTS, ROWS, E), BF)]
    encoded = whole(
        encode_kernel,
        [*fetched, context, core_swap(context)],
        [slots(SLOTS)],
        "encode",
        [look],
        scratch=scratch,
    )[0]
    outs = [jax.ShapeDtypeStruct((rows, query_weight.shape[1]), BF)]
    arrays = [tok_stack, core_swap(tok_stack), query_weight]
    queries = whole(queries_kernel, arrays, outs, "queries", after=[encoded])[0]
    attention = attend(with_swaps(chip_blocks(encoded)), queries, key_weight, value_weight)
    return project(with_swaps(chip_blocks(attention)), output_weight)


def solution(mesh):
    placed = (
        P("seq", "head"),
        P("seq", None),
        P("seq", None),
        P("seq", None, None),
        P("head", None),
        P(None, "head"),
        P(None, "head"),
        P(None, "head"),
        P(None, "head"),
    )
    return jax.shard_map(
        local, mesh=mesh, in_specs=placed, out_specs=P("seq", "head"), check_vma=False
    )
```

```python
import functools
import math

import jax
import jax.numpy as jnp
from jax import lax
from jax.experimental import pallas as pl
from jax.experimental.pallas import tpu as pltpu
from jax.sharding import PartitionSpec as P

HD = 128
E = 896
CL = 64
NL = 128
KN = 2
EHD = 128
NX, NZ, NY, NC = 4, 8, 4, 2
NS = NX * NZ
NH = NY * NC
STORE_DEV = 16
SLOTS = 8
ROWS = NL // NH
PIECES = ((0, 512), (512, 896))
BF = jnp.bfloat16
F32 = jnp.float32

VMEM = pl.BlockSpec(memory_space=pltpu.VMEM)
SMEM = pl.BlockSpec(memory_space=pltpu.SMEM)
ANY = pl.BlockSpec(memory_space=pl.ANY)


def without(count, at, kernel, *refs):
    kernel(*refs[:at], *refs[at + count :])


def whole(body, arrays, outs, name, lists=(), after=(), scratch=(), limit=8):
    size = sum(a.size * a.dtype.itemsize for a in [*arrays, *outs])
    return pl.pallas_call(
        functools.partial(without, len(after), len(lists) + len(arrays), body),
        out_shape=outs,
        in_specs=[SMEM] * len(lists) + [VMEM] * len(arrays) + [ANY] * len(after),
        out_specs=[VMEM] * len(outs),
        scratch_shapes=scratch,
        compiler_params=pltpu.CompilerParams(vmem_limit_bytes=limit * 2**20),
        cost_estimate=pl.CostEstimate(flops=0, bytes_accessed=size, transcendentals=0),
        name=name,
    )(*lists, *arrays, *after)


def y_shift(a, r):
    pairs = [(y * NC + c, ((y + r) % NY) * NC + c) for y in range(NY) for c in range(NC)]
    return lax.ppermute(a, "head", pairs)


def core_swap(a):
    return lax.ppermute(a, "head", [(h, h ^ 1) for h in range(NH)])


def z_shift(a, r):
    pairs = [(x * NZ + z, x * NZ + (z + r) % NZ) for x in range(NX) for z in range(NZ)]
    return lax.ppermute(a, "seq", pairs)


def x_shift(a, r):
    pairs = [(x * NZ + z, ((x + r) % NX) * NZ + z) for x in range(NX) for z in range(NZ)]
    return lax.ppermute(a, "seq", pairs)


def far_shift(a):
    pairs = []
    for x in range(NX):
        for z in range(NZ):
            for h in range(NH):
                step = 2 if h % NC else -2
                pairs.append(((x * NZ + z) * NH + h, (x * NZ + (z + step) % NZ) * NH + h))
    return lax.ppermute(a, ("seq", "head"), pairs)


def chip_blocks(a):
    two, one, three = [y_shift(a, r) for r in (2, 1, 3)]
    return [a, one, two, three]


def chip_blocks_in_turn(a):
    one, three = y_shift(a, 1), y_shift(a, 3)
    return [a, one, y_shift(one, 1), three]


def with_swaps(blocks):
    return [b for own in blocks for b in (own, core_swap(own))]


def source_head(k):
    head = lax.axis_index("head")
    y, c = head // NC, head % NC
    return ((y - k // NC + NY) % NY) * NC + (c if k % NC == 0 else 1 - c)


def partial_kernel(tokens, weight, mine, theirs):
    c = lax.axis_index("head") % NC
    total = jnp.dot(tokens[...], weight[...], preferred_element_type=F32)
    parts = total.reshape(NY, NC, -1, E)
    mine[...] = jnp.where(c == 0, parts[:, 0], parts[:, 1])
    theirs[...] = jnp.where(c == 0, parts[:, 1], parts[:, 0])


def chip_sum_kernel(mine, received, *outs):
    y = lax.axis_index("head") // NC
    for r, out in enumerate(outs):
        to = (y + r) % NY
        out[...] = mine[to] + received[to]


def pack_kernel(one, two, three, four, tokens, out):
    rows = tokens.shape[0]
    part = one.shape[0]
    out[:rows] = tokens[...]
    context = (one[...] + two[...] + three[...] + four[...]).astype(BF)
    for i, (first, last) in enumerate(PIECES):
        start = rows + i * part
        out[start : start + part, : last - first] = context[:, first:last]


def half_sums(tokens, weight, y, c):
    rows = tokens.shape[0]
    part = rows // NH
    parts = jnp.dot(tokens, weight, preferred_element_type=F32).reshape(NY, NC, part, E)
    mine = lax.dynamic_index_in_dim(parts, c, axis=1, keepdims=False)
    theirs = lax.dynamic_index_in_dim(parts, 1 - c, axis=1, keepdims=False)
    return mine, core_swap(theirs)


def packed_context(halves, tokens, after, after_sum):
    rows, width = tokens.shape
    part = rows // NH
    outs = [jax.ShapeDtypeStruct((part, E), F32)] * NY
    own, *sent = whole(chip_sum_kernel, list(halves), outs, "chip_sum", after=after)
    received = [y_shift(sent[r - 1], r) for r in (1, 3, 2)]
    out = jax.ShapeDtypeStruct((rows + len(PIECES) * part, width), BF)
    return whole(pack_kernel, [own, *received, tokens], [out], "pack", after=after_sum)[0]


def z_lists(lists, shifts):
    for r in shifts:
        lists = jnp.concatenate([lists, z_shift(lists, r)], axis=0)
    return lists


def slab_of(store):
    own = lax.dynamic_slice_in_dim(store, lax.axis_index("head") * ROWS, ROWS, axis=1)
    one, three, two = [x_shift(own, r) for r in (1, 3, 2)]
    return [own, one, two, three]


def locate(value):
    seq = lax.axis_index("seq")
    shard = value // STORE_DEV
    away = (shard % NZ - seq % NZ + NZ) % NZ
    back = (seq // NZ - shard // NZ + NX) % NX
    return away, back, value % STORE_DEV


def from_slab(slab, back, row):
    value = slab[0][row]
    for r in range(1, NX):
        value = jnp.where(back == r, slab[r][row], value)
    return value


def first_kernel(look, s0, s1, s2, s3, minus, plus, far):
    slab = (s0, s1, s2, s3)
    for k, out, base in [
        (1, minus, 0),
        (3, minus, SLOTS),
        (7, plus, 0),
        (5, plus, SLOTS),
        (4, far, 0),
    ]:
        for q in range(SLOTS):
            _, back, row = locate(look[k, q])
            out[base + q] = from_slab(slab, back, row)


def second_kernel(look, s0, s1, s2, s3, minus_in, plus_in, far_in, minus, plus, mine):
    slab = (s0, s1, s2, s3)
    for k, out, near, d in [(2, minus, minus_in, 1), (6, plus, plus_in, 7)]:
        for q in range(SLOTS):
            away, back, row = locate(look[k, q])
            value = jnp.where(away == d, near[SLOTS + q], far_in[q])
            out[q] = jnp.where(away == 0, from_slab(slab, back, row), value)
    for q in range(SLOTS):
        away, back, row = locate(look[0, q])
        value = jnp.where(away == 1, minus_in[q], plus_in[q])
        mine[q] = jnp.where(away == 0, from_slab(slab, back, row), value)


def slots(count):
    return jax.ShapeDtypeStruct((count, ROWS, E), BF)


def first_hop(slab, look):
    outs = [slots(2 * SLOTS), slots(2 * SLOTS), slots(SLOTS)]
    return whole(first_kernel, slab, outs, "first", [look])


def sent_on(slots_out):
    minus, plus, far = slots_out
    return [z_shift(minus, -1), z_shift(plus, 1), far_shift(far)]


def second_hop(slab, look, arrays):
    return whole(second_kernel, slab + arrays, [slots(SLOTS)] * 3, "second", [look])


def stack_kernel(*refs):
    blocks, (tokens, context) = refs[:NY], refs[NY:]
    rows, part = tokens.shape[1], context.shape[1]
    for r, block in enumerate(blocks):
        tokens[r] = block[:rows]
        for i, (first, last) in enumerate(PIECES):
            at = rows + i * part
            context[r, :, first:last] = block[at : at + part, : last - first]


def queries_kernel(own, other, w, out):
    blocks = [(own, other)[k % NC].at[k // NC] for k in range(NH)]
    depth = w.shape[0] // NH
    total = None
    for k in range(NH):
        start = pl.multiple_of(source_head(k) * depth, depth)
        dot = jnp.dot(blocks[k][...], w[pl.ds(start, depth), :], preferred_element_type=F32)
        total = dot if total is None else total + dot
    out[...] = total.astype(out.dtype)


def encode_kernel(look, mine, ahead_in, behind_in, ctx, other_ctx, out, nb):
    width = nb.shape[-1]
    core = lax.axis_index("head") % NC
    for q in range(SLOTS):
        away, _, _ = locate(look[0, q])
        ahead = (away == 2) | (away == 3) | ((away == 4) & (core == 0))
        near = (away == 0) | (away == 1) | (away == NZ - 1)
        nb[q] = jnp.where(near, mine[q], jnp.where(ahead, ahead_in[q], behind_in[q]))
    heads = range(width // EHD)
    for r in range(NY):
        span = source_head(NC * r) // NC
        context = jnp.concatenate([ctx[r], other_ctx[r]], axis=0)
        rows = nb[pl.ds(span * KN, KN)].reshape(KN * ROWS, width)
        scores = jnp.concatenate(
            [
                lax.dot_general(
                    rows[:, g * EHD : (g + 1) * EHD],
                    context[:, g * EHD : (g + 1) * EHD],
                    (((1,), (1,)), ((), ())),
                    preferred_element_type=F32,
                )
                for g in heads
            ],
            axis=0,
        ) * (1.0 / math.sqrt(EHD))
        weights = jnp.exp(scores - jnp.max(scores, axis=1, keepdims=True))
        weights = (weights / jnp.sum(weights, axis=1, keepdims=True)).astype(BF)
        mixed = jnp.concatenate(
            [
                jnp.dot(
                    weights[g * KN * ROWS : (g + 1) * KN * ROWS],
                    context[:, g * EHD : (g + 1) * EHD],
                    preferred_element_type=F32,
                )
                for g in heads
            ],
            axis=1,
        )
        encoded = (rows.astype(F32) + mixed).astype(BF)
        out[pl.ds(span * KN, KN)] = encoded.reshape(KN, ROWS, width)


def attend_kernel(*refs):
    blocks = refs[:NH]
    q_hbm, wk_hbm, wv_hbm, out, rows, q, wk, wv, sems = refs[NH:]
    spans = rows.shape[0]
    pairs = [(block, rows.at[:, k]) for k, block in enumerate(blocks)]
    pairs += [(wk_hbm, wk), (wv_hbm, wv), (q_hbm, q)]
    copies = [pltpu.make_async_copy(a, b, sems.at[i]) for i, (a, b) in enumerate(pairs)]
    for copy in copies:
        copy.start()
    for copy in copies:
        copy.wait()
    flat = rows[...].reshape(spans * KN * NL, E)
    keys = jnp.dot(flat, wk[...], preferred_element_type=F32).astype(BF)
    values = jnp.dot(flat, wv[...], preferred_element_type=F32).astype(BF)
    heads = q.shape[1] // HD
    span_rows = KN * NL
    units = [(s, h) for s in range(spans) for h in range(heads)]
    scores = jnp.concatenate(
        [
            lax.dot_general(
                q[s * CL : (s + 1) * CL, h * HD : (h + 1) * HD],
                keys[s * span_rows : (s + 1) * span_rows, h * HD : (h + 1) * HD],
                (((1,), (1,)), ((), ())),
                preferred_element_type=F32,
            )
            for s, h in units
        ],
        axis=0,
    ) * (1.0 / math.sqrt(HD))
    weights = jnp.exp(scores - jnp.max(scores, axis=1, keepdims=True))
    weights = (weights / jnp.sum(weights, axis=1, keepdims=True)).astype(BF)
    for i, (s, h) in enumerate(units):
        out[s * CL : (s + 1) * CL, h * HD : (h + 1) * HD] = jnp.dot(
            weights[i * CL : (i + 1) * CL],
            values[s * span_rows : (s + 1) * span_rows, h * HD : (h + 1) * HD],
            preferred_element_type=F32,
        ).astype(BF)


def attend(blocks, queries, key_weight, value_weight):
    tokens, width = queries.shape
    spans = tokens // CL
    blocks = [b.reshape(spans, KN * ROWS, E) for b in blocks]
    arrays = [queries, key_weight, value_weight]
    return pl.pallas_call(
        attend_kernel,
        out_shape=jax.ShapeDtypeStruct((tokens, width), BF),
        in_specs=[ANY] * (NH + 3),
        out_specs=VMEM,
        scratch_shapes=[
            pltpu.VMEM((spans, NH, KN * ROWS, E), BF),
            *[pltpu.VMEM(a.shape, BF) for a in arrays],
            pltpu.SemaphoreType.DMA((NH + 3,)),
        ],
        compiler_params=pltpu.CompilerParams(vmem_limit_bytes=14 * 2**20),
        cost_estimate=pl.CostEstimate(
            flops=4 * spans * KN * NL * E * width,
            bytes_accessed=2 * (spans * KN * NL * E + 2 * E * width + 2 * tokens * width),
            transcendentals=0,
        ),
        name="attend",
    )(*blocks, *arrays)


def project_kernel(*refs):
    blocks, w, out = refs[:NH], refs[NH], refs[NH + 1]
    depth = w.shape[0] // NH
    total = None
    for k in range(NH):
        start = pl.multiple_of(source_head(k) * depth, depth)
        dot = jnp.dot(blocks[k][...], w[pl.ds(start, depth), :], preferred_element_type=F32)
        total = dot if total is None else total + dot
    out[...] = total.astype(out.dtype)


def project(blocks, w):
    rows = blocks[0].shape[0]
    return pl.pallas_call(
        project_kernel,
        out_shape=jax.ShapeDtypeStruct((rows, w.shape[1]), BF),
        in_specs=[VMEM] * (NH + 1),
        out_specs=VMEM,
        compiler_params=pltpu.CompilerParams(vmem_limit_bytes=8 * 2**20),
        cost_estimate=pl.CostEstimate(
            flops=2 * rows * w.size, bytes_accessed=4 * w.size, transcendentals=0
        ),
        name="project",
    )(*blocks, w)


def local(
    tokens,
    neighbour_shard,
    neighbour_row,
    store_rows,
    context_weight,
    query_weight,
    key_weight,
    value_weight,
    output_weight,
):
    rows = tokens.shape[0]
    head = lax.axis_index("head")
    slab = slab_of(store_rows)
    own = (neighbour_shard * STORE_DEV + neighbour_row).reshape(1, SLOTS)
    look = z_lists(own, (1, 2, 4))
    halves = half_sums(tokens, context_weight, head // NC, head % NC)
    sent = first_hop(slab, look)
    arrays = sent_on(sent)
    minus, plus, mine = second_hop(slab, look, arrays)
    fetched = [mine, z_shift(minus, -2), z_shift(plus, 2)]
    packed = packed_context(halves, tokens, (), arrays[:2])
    chips = chip_blocks(packed)
    outs = [
        jax.ShapeDtypeStruct((NY, *tokens.shape), BF),
        jax.ShapeDtypeStruct((NY, rows // NH, E), BF),
    ]
    tok_stack, context = whole(stack_kernel, chips, outs, "stack", after=fetched[1:])
    scratch = [pltpu.VMEM((SLOTS, ROWS, E), BF)]
    encoded = whole(
        encode_kernel,
        [*fetched, context, core_swap(context)],
        [slots(SLOTS)],
        "encode",
        [look],
        scratch=scratch,
    )[0]
    outs = [jax.ShapeDtypeStruct((rows, query_weight.shape[1]), BF)]
    arrays = [tok_stack, core_swap(tok_stack), query_weight]
    queries = whole(queries_kernel, arrays, outs, "queries", after=[encoded])[0]
    attention = attend(with_swaps(chip_blocks(encoded)), queries, key_weight, value_weight)
    return project(with_swaps(chip_blocks(attention)), output_weight)


def solution(mesh):
    placed = (
        P("seq", "head"),
        P("seq", None),
        P("seq", None),
        P("seq", None, None),
        P("head", None),
        P(None, "head"),
        P(None, "head"),
        P(None, "head"),
        P(None, "head"),
    )
    return jax.shard_map(
        local, mesh=mesh, in_specs=placed, out_specs=P("seq", "head"), check_vma=False
    )
```
